256 devices in a mesh: dp: 64 (over z, y, core), shard: 4 (over x).
Axes of the slice: x: 4, y: 4, z: 8, core: 2. Of those that a mesh axis runs over, the one named last changes fastest.
Arguments:
- gradients: float32 [1024, 256, 256], P('dp', 'shard'), may hold values from -6 to 6
- left_stats: float32 [1024, 256, 256], P('dp', 'shard'), may hold values from -3 to 100, as said below
- right_stats: float32 [1024, 256, 256], P('dp', 'shard'), may hold values from -3 to 100, as said below
- left_roots: float32 [1024, 256, 256], P('dp', 'shard'), may hold values from -0.1 to 3, as said below
- right_roots: float32 [1024, 256, 256], P('dp', 'shard'), may hold values from -0.1 to 3, as said below
- due_factors: int32 [1024], replicated, may hold values from 0 to 2047, as said below
- block_owner: int32 [1024], replicated, may hold values from 0 to 1023, as said below
Outputs:
- new_left: float32 [1024, 256, 256], P('dp', 'shard')
- new_right: float32 [1024, 256, 256], P('dp', 'shard')
- new_left_roots: float32 [1024, 256, 256], P('dp', 'shard')
- new_right_roots: float32 [1024, 256, 256], P('dp', 'shard')
- update: float32 [1024, 256, 256], P('dp', 'shard')
The draws below stay inside these ranges and needn't reach their ends.
Inputs may be any that keep to these rules, and one draw needn't show every extreme that they name: `block_owner`: each of the 1024 storage slots appears once; slot s is kept by index s // 16 of dp. `due_factors`: distinct values 2 b + side for block b, side 0 naming the left factor and 1 the right; the due factors of the blocks kept by one index of dp number at most 32, and exactly that many on some index. `left_stats`: each block is symmetric positive definite. `right_stats`: each block is symmetric positive definite. `left_roots`: each block is symmetric positive definite. `right_roots`: each block is symmetric positive definite.
All inputs are finite; a program needn't handle non-finite values.
Results may differ from the reference program's by a relative error of at most 0.00017.
Values sent between devices are 32-bit elements; how exact they have to be, the bound alone decides.
A program may use at most 64 MiB of HBM per device.

```python
import math
import jax
import jax.numpy as jnp
from jax import lax

BLOCK = 256
BLK_DEV = 16
ITERS = 10
NB = 1024
NDUE = 1024


def definite(key, low, high):
    diag_key, size_key, sign_key = jax.random.split(key, 3)
    extent = BLOCK
    scales = jnp.exp(jax.random.uniform(diag_key, (NB, extent), jnp.float32, math.log(low), math.log(high)))
    magnitudes = 0.5 + 0.5 * jax.random.uniform(size_key, (NB, extent, extent), jnp.float32)
    sign_values = jnp.where(jax.random.bernoulli(sign_key, 0.5, (NB, extent, extent)), 1.0, -1.0)
    raw_values = magnitudes * sign_values
    row_index = lax.broadcasted_iota(jnp.int32, (extent, extent), 0)
    col_index = lax.broadcasted_iota(jnp.int32, (extent, extent), 1)
    mirrored = jnp.where(row_index < col_index, raw_values, jnp.swapaxes(raw_values, 1, 2))
    coupling = jnp.where(row_index == col_index, 1.0, 0.9 / (extent - 1) * mirrored)
    root_scale = jnp.sqrt(scales)
    return (root_scale[:, :, None] * coupling * root_scale[:, None, :]).astype(jnp.float32)


def storage_slots(key):
    return jax.random.permutation(jax.random.fold_in(key, 11), NB).astype(jnp.int32)


def draw_block_owner(key, part):
    slot_table = storage_slots(key)
    return slot_table


def draw_due_factors(key, part):
    slot_table = storage_slots(key)
    key = jax.random.fold_in(key, 2)
    busy_key, score_key = jax.random.split(key)
    factor_total = 2 * NB
    per_group = 2 * BLK_DEV
    group_count = NB // BLK_DEV
    busy_count = max(1, NDUE // (2 * per_group))
    shuffled = jax.random.permutation(busy_key, group_count)
    busy_flag = jnp.zeros((group_count,), jnp.int32).at[shuffled[:busy_count]].set(1)
    storage = jnp.arange(factor_total, dtype=jnp.int32)
    busy_of = jnp.take(busy_flag, storage // per_group)
    scores = jax.random.randint(score_key, (factor_total,), 0, 2 ** 17) * factor_total + storage + busy_of * 2 ** 30
    picked = lax.top_k(scores, NDUE)[1].astype(jnp.int32)
    inverse = jnp.argsort(slot_table, stable=True).astype(jnp.int32)
    blocks = jnp.take(inverse, picked // 2)
    return (2 * blocks + picked % 2).astype(jnp.int32)


def draw_left_stats(key, part):
    key = jax.random.fold_in(key, 3)
    return definite(key, 0.1, 100.0)


def draw_right_stats(key, part):
    key = jax.random.fold_in(key, 4)
    return definite(key, 0.1, 100.0)


def draw_left_roots(key, part):
    key = jax.random.fold_in(key, 5)
    return definite(key, 0.1, 3.0)


def draw_right_roots(key, part):
    key = jax.random.fold_in(key, 6)
    return definite(key, 0.1, 3.0)


def block_scale(stream_key, shape, cuts, least, largest):
    loudness, own = 1.0, jax.random.fold_in(stream_key, 6)
    for dim, shards_of in cuts:
        heights = jnp.exp(jax.random.uniform(jax.random.fold_in(own, dim), (shards_of,), jnp.float32, least / len(cuts), largest / len(cuts)))
        loudness = loudness * jnp.repeat(heights, shape[dim] // shards_of).reshape([-1 if axis == dim else 1 for axis in range(len(shape))])
    return loudness


def centred(stream_key, shape, scale, reach, cuts=(), kind=jnp.bfloat16):
    result = scale * jax.random.normal(stream_key, shape, jnp.float32)
    if cuts:
        result = result * block_scale(stream_key, shape, cuts, -0.22, 0.18)
    return jnp.clip(result, -reach, reach).astype(kind)


def setup_inputs(seed: int = 0) -> dict:
    streams_of = jax.random.split(jax.random.key(seed), 8)
    gradients = centred(streams_of[0], (NB, BLOCK, BLOCK), 1.0, 6.0, ((0, 64), (1, 4)), jnp.float32)
    left_stats = draw_left_stats(jax.random.fold_in(streams_of[7], 71), 0)
    right_stats = draw_right_stats(jax.random.fold_in(streams_of[7], 71), 0)
    left_roots = draw_left_roots(jax.random.fold_in(streams_of[7], 71), 0)
    right_roots = draw_right_roots(jax.random.fold_in(streams_of[7], 71), 0)
    due_factors = draw_due_factors(jax.random.fold_in(streams_of[7], 71), 0)
    block_owner = draw_block_owner(jax.random.fold_in(streams_of[7], 71), 0)
    return dict(gradients=gradients, left_stats=left_stats, right_stats=right_stats, left_roots=left_roots, right_roots=right_roots, due_factors=due_factors, block_owner=block_owner)


STAT_DECAY = 0.95
PRECISE = lax.Precision.HIGHEST

def newton_root(matrices):
    extent = matrices.shape[-1]
    identity = jnp.eye(extent, dtype=jnp.float32)
    frobenius = jnp.sqrt(lax.optimization_barrier(jnp.sum(matrices * matrices, axis=(-2, -1))))
    matrix = matrices / frobenius[..., None, None]
    iterate = identity * (frobenius ** (-0.25))[..., None, None]

    def newton_step(counter, carry):
        iterate, matrix = carry
        factor = (5.0 * identity - matrix) * 0.25
        iterate = jnp.einsum('...ij,...jk->...ik', iterate, factor, precision=PRECISE)
        square = jnp.einsum('...ij,...jk->...ik', factor, factor, precision=PRECISE)
        fourth = jnp.einsum('...ij,...jk->...ik', square, square, precision=PRECISE)
        matrix = jnp.einsum('...ij,...jk->...ik', fourth, matrix, precision=PRECISE)
        return (iterate, matrix)
    iterate, matrix = lax.fori_loop(0, ITERS, newton_step, (iterate, matrix))
    return iterate

def reference(gradients, left_stats, right_stats, left_roots, right_roots, due_factors, block_owner):
    left_gram = jnp.einsum('bik,bjk->bij', gradients, gradients, precision=PRECISE)
    right_gram = jnp.einsum('bki,bkj->bij', gradients, gradients, precision=PRECISE)
    new_left = STAT_DECAY * left_stats + (1.0 - STAT_DECAY) * left_gram
    new_right = STAT_DECAY * right_stats + (1.0 - STAT_DECAY) * right_gram
    side_of = (due_factors % 2).astype(jnp.int32)
    slot_of = jnp.take(block_owner, (due_factors // 2).astype(jnp.int32)).astype(jnp.int32)
    chosen = jnp.where((side_of == 0)[:, None, None], jnp.take(new_left, slot_of, axis=0), jnp.take(new_right, slot_of, axis=0))
    root_stack = newton_root(chosen)
    block_count = left_roots.shape[0]
    left_target = jnp.where(side_of == 0, slot_of, block_count).astype(jnp.int32)
    right_target = jnp.where(side_of == 1, slot_of, block_count).astype(jnp.int32)
    new_left_roots = left_roots.at[left_target].set(root_stack, mode='drop')
    new_right_roots = right_roots.at[right_target].set(root_stack, mode='drop')
    middle = jnp.einsum('bik,bkj->bij', new_left_roots, gradients, precision=PRECISE)
    update = jnp.einsum('bik,bkj->bij', middle, new_right_roots, precision=PRECISE)
    return (new_left, new_right, new_left_roots, new_right_roots, update)
```

```python
import functools

import jax
import jax.numpy as jnp
from jax import lax
from jax.experimental import pallas as pl
from jax.experimental.pallas import tpu as pltpu
from jax.sharding import PartitionSpec as P

ITERS = 10
STAT_DECAY = 0.95
MESH = pl.DeviceIdType.MESH
VMEM_LIMIT = 63 * 1024 * 1024
F32 = jnp.float32
BF16 = jnp.bfloat16


def mm(a, b):
    return jnp.dot(a, b, precision=lax.Precision.HIGH, preferred_element_type=F32)


def kernel(
    n,
    g, ls, rs, lr, rr, due, own,
    stats_out, roots_out,
    duev, ownv, gf, st, rt, sel, spk, pk, p, gg, rg, out, mk,
    fg, fs, fgg, fo,
    spread, mat, root,
    load_sem, own_sem, done_sem,
    g_send, g_recv, s_send, s_recv, q_send, q_recv, o_send, o_recv,
):
    blocks, quarter, extent = g.shape
    each = blocks // n
    half = extent // 2
    me = lax.axis_index("shard")
    group = lax.axis_index("dp")
    right = lax.rem(me + 1, n)
    left = lax.rem(me + n - 1, n)
    opposite = lax.rem(me + 2, n)
    sides = ((right, left), (left, right))

    def rows(index):
        return pl.ds(pl.multiple_of(index * quarter, quarter), quarter)

    def cols(d):
        return pl.ds(d * half, half)

    def remote(src, dst, send, recv, device):
        return pltpu.make_async_remote_copy(
            src_ref=src, dst_ref=dst, send_sem=send, recv_sem=recv,
            device_id=(group, device), device_id_type=MESH,
        )

    def g_copy(d, stage, j):
        device, origin = sides[d]
        return remote(*(
            (g.at[opposite * each + j, :, cols(d)], fg.at[d, j], g_send.at[d, 0, j], g_recv.at[d, 0, j], device),
            (g.at[device * each + j], gf.at[j, rows(me), :], g_send.at[d, 1, j], g_recv.at[d, 1, j], device),
            (fg.at[d, j], gf.at[j, rows(origin), cols(d)], g_send.at[d, 2, j], g_recv.at[d, 2, j], device),
        )[stage])

    def s_copy(d, stage, j):
        device, origin = sides[d]
        return remote(*(
            (spk.at[opposite * each + j, d], fs.at[d, j], s_send.at[d, 0, j], s_recv.at[d, 0, j], device),
            (spk.at[device * each + j], pk.at[me, j], s_send.at[d, 1, j], s_recv.at[d, 1, j], device),
            (fs.at[d, j], pk.at[origin, j, d], s_send.at[d, 2, j], s_recv.at[d, 2, j], device),
        )[stage])

    def q_copy(d, stage, j):
        device, origin = sides[d]
        return remote(*(
            (gg.at[:, j, rows(opposite), cols(d)], fgg.at[d, j], q_send.at[d, 0, j], q_recv.at[d, 0, j], device),
            (gg.at[:, j, rows(device), :], rg.at[:, me * each + j], q_send.at[d, 1, j], q_recv.at[d, 1, j], device),
            (fgg.at[d, j], rg.at[:, origin * each + j, :, cols(d)], q_send.at[d, 2, j], q_recv.at[d, 2, j], device),
        )[stage])

    def o_copy(d, stage, j):
        device, origin = sides[d]
        return remote(*(
            (out.at[:, j, rows(opposite), cols(d)], fo.at[d, j], o_send.at[d, 0, j], o_recv.at[d, 0, j], device),
            (out.at[:, j, rows(device), :], roots_out.at[:, me * each + j], o_send.at[d, 1, j], o_recv.at[d, 1, j], device),
            (fo.at[d, j], roots_out.at[:, origin * each + j, :, cols(d)], o_send.at[d, 2, j], o_recv.at[d, 2, j], device),
        )[stage])

    def begin(copy, j):
        for stage in (0, 1):
            for d in (0, 1):
                copy(d, stage, j).start()

    def forward(copy, j):
        for d in (0, 1):
            copy(d, 0, j).wait_recv()
            copy(d, 2, j).start()

    def arrived(copy, j):
        for d in (0, 1):
            for stage in (1, 2):
                copy(d, stage, j).wait_recv()

    def o_own(j):
        return pltpu.make_async_copy(
            out.at[:, j, rows(me), :], roots_out.at[:, me * each + j], done_sem.at[0, j]
        )

    def q_own(j):
        return pltpu.make_async_copy(
            gg.at[:, j, rows(me), :], rg.at[:, me * each + j], done_sem.at[1, j]
        )

    loads = [
        pltpu.make_async_copy(ref, place, load_sem.at[i])
        for i, (ref, place) in enumerate(
            ((due, duev), (own, ownv), (ls, st.at[0]), (rs, st.at[1]), (lr, rt.at[0]), (rr, rt.at[1]))
        )
    ]
    own_rows = pltpu.make_async_copy(
        g.at[pl.ds(me * each, each)], gf.at[:, rows(me), :], own_sem.at[0]
    )
    for load in loads:
        load.start()

    barrier = pltpu.get_barrier_semaphore()
    for device in (left, right):
        pl.semaphore_signal(barrier, inc=1, device_id=(group, device), device_id_type=MESH)
    pl.semaphore_wait(barrier, 2)

    begin(g_copy, 0)
    begin(g_copy, 1)
    own_rows.start()

    total = own.shape[1]
    for load in loads[:2]:
        load.wait()
    slots = group * blocks + lax.broadcasted_iota(jnp.int32, (blocks, total), 0)
    numbers = lax.broadcasted_iota(jnp.int32, (blocks, total), 1)
    stored = jnp.where(ownv[...] == slots, numbers, 0).astype(F32)
    number = jnp.sum(stored, axis=1, keepdims=True)
    entries = duev[...].astype(F32)
    for side in (0, 1):
        hit = jnp.where(entries == 2.0 * number + side, 1.0, 0.0)
        flag = jnp.max(hit, axis=1, keepdims=True)
        mk[side] = jnp.broadcast_to(flag, (blocks, half))

    for load in loads[2:]:
        load.wait()

    low_lanes = lax.broadcasted_iota(jnp.int32, (quarter, half), 1) < quarter

    @pl.loop(0, blocks)
    def _(b):
        second = lax.rem(jnp.where(b // each == right, me + 2, me + 1), n)
        for side in (0, 1):
            flag = mk[side, pl.ds(b, 1), :] > 0.5
            halves = []
            for d in (0, 1):
                value = jnp.where(
                    flag,
                    st[side, b, :, d * half:(d + 1) * half],
                    rt[side, b, :, d * half:(d + 1) * half],
                )
                sel[side, b, :, d * half:(d + 1) * half] = value
                halves.append(value)
            low = jnp.where(me // 2 == 0, halves[0], halves[1])
            low = jnp.where(lax.rem(me, 2) == 0, low, pltpu.roll(low, quarter, 1))
            high = jnp.where(second // 2 == 0, halves[0], halves[1])
            high = jnp.where(lax.rem(second, 2) == 1, high, pltpu.roll(high, quarter, 1))
            spk[b, side] = jnp.where(low_lanes, low, high)

    begin(s_copy, 0)
    begin(s_copy, 1)
    forward(g_copy, 0)
    forward(s_copy, 0)
    begin(g_copy, 2)
    begin(s_copy, 2)
    forward(g_copy, 1)
    forward(s_copy, 1)
    begin(g_copy, 3)
    begin(s_copy, 3)
    own_rows.wait()

    row_ids = lax.broadcasted_iota(jnp.int32, (extent, extent), 0)
    col_ids = lax.broadcasted_iota(jnp.int32, (extent, extent), 1)
    diagonal = row_ids == col_ids
    mat[...] = jnp.zeros_like(mat)
    root[...] = jnp.zeros_like(root)

    def partner(row):
        return lax.rem(row + jnp.where(row == left, 2, 1), n)

    def gram(j):
        arrived(g_copy, j)
        straight = gf[j]
        turned = straight.T
        gg[0, j] = mm(straight, turned)
        gg[1, j] = mm(turned, straight)
        begin(q_copy, j)
        q_own(j).start()

    def prepare(j, chain):
        arrived(s_copy, j)
        row_part, col_part = row_ids // quarter, col_ids // quarter
        other = lax.rem(row_part + jnp.where(row_part == left, 2, 1), n)
        known = (row_part == me) | (row_part == col_part) | (col_part == other)
        for i in (0, 1):
            for row in range(n):
                second = partner(row)
                packed = pk[row, j, i]
                turned_round = pltpu.roll(packed, quarter, 1)
                low = packed if row % 2 == 0 else turned_round
                high = jnp.where(lax.rem(second, 2) == 1, packed, turned_round)
                for d in (0, 1):
                    part = 2 * d + jnp.where(low_lanes, 0, 1)
                    value = jnp.where(part == row, low, jnp.where(part == second, high, 0.0))
                    value = jnp.where(
                        me == row, sel[i, me * each + j, :, d * half:(d + 1) * half], value
                    )
                    spread[i, row * quarter:(row + 1) * quarter, d * half:(d + 1) * half] = value
            whole = spread[i]
            whole = jnp.where(known, whole, whole.T)
            p[i, j] = whole
            chosen = STAT_DECAY * whole + (1.0 - STAT_DECAY) * gg[i, j]
            frobenius = jnp.sqrt(jnp.sum(chosen * chosen, keepdims=True))
            mat[chain + i] = chosen / frobenius
            root[chain + i] = jnp.where(diagonal, 1.0 / jnp.sqrt(jnp.sqrt(frobenius)), 0.0)

    def finish(j, chain):
        for i in (0, 1):
            flag = mk[i, pl.ds(me * each + j, 1), :] > 0.5
            for d in (0, 1):
                out[i, j, :, d * half:(d + 1) * half] = jnp.where(
                    flag,
                    root[chain + i, :, d * half:(d + 1) * half],
                    p[i, j, :, d * half:(d + 1) * half],
                )
        out[2, j] = mm(mm(out[0, j], gf[j]), out[1, j])
        begin(o_copy, j)
        o_own(j).start()

    gram(0)

    pairs = ITERS // 2
    lag = 2
    chains = range(4)

    @pl.loop(0, 2 * pairs + lag)
    def _(t):
        @pl.when(lax.rem(t, pairs) == 0)
        def _():
            @pl.when(t < 2 * pairs)
            def _():
                prepare(2 * (t // pairs), 0)

        @pl.when(lax.rem(t, pairs) == lag)
        def _():
            prepare(2 * (t // pairs) + 1, 2)

        factor = [jnp.where(diagonal, 1.25, 0.0) - 0.25 * mat[i] for i in chains]
        square = [mm(f, f) for f in factor]
        fourth = [mm(s, s) for s in square]
        term = [mm(q, 5.0 * f - 4.0 * s) for q, f, s in zip(fourth, factor, square)]
        joint = [1.25 * f - 0.25 * u for f, u in zip(factor, term)]
        product = [mm(root[i], joint[i]) for i in chains]
        for i in chains:
            root[i] = product[i]
        square = [mm(f, f) for f in joint]
        fourth = [mm(s, s) for s in square]
        matrix = [mm(fourth[i], mat[i]) for i in chains]
        for i in chains:
            mat[i] = matrix[i]

        @pl.when(lax.rem(t, pairs) == pairs - 1)
        def _():
            finish(2 * (t // pairs), 0)

        @pl.when(lax.rem(t, pairs) == lag - 1)
        def _():
            @pl.when(t >= pairs)
            def _():
                finish(2 * (t // pairs) - 1, 2)

        def at(step, *actions):
            @pl.when(t == step)
            def _():
                for action, *rest in actions:
                    action(*rest)

        at(0, (forward, g_copy, 2), (forward, s_copy, 2), (gram, 1))
        at(1, (forward, g_copy, 3), (forward, s_copy, 3))
        at(2, (forward, q_copy, 0), (gram, 2))
        at(3, (gram, 3))
        at(4, (forward, q_copy, 1))
        at(6, (forward, q_copy, 2))
        at(7, (forward, q_copy, 3))
        at(8, (forward, o_copy, 0))
        at(10, (forward, o_copy, 1))

    forward(o_copy, 2)
    forward(o_copy, 3)

    @pl.loop(0, each)
    def _(j):
        q_own(j).wait()
        arrived(q_copy, j)

    @pl.loop(0, blocks)
    def _(b):
        for side in (0, 1):
            rg[side, b] = STAT_DECAY * st[side, b] + (1.0 - STAT_DECAY) * rg[side, b]

    statistics = pltpu.make_async_copy(rg, stats_out, own_sem.at[1])
    statistics.start()

    @pl.loop(0, each)
    def _(j):
        for copy in (g_copy, s_copy, q_copy, o_copy):
            for d in (0, 1):
                for stage in (0, 1, 2):
                    copy(d, stage, j).wait_send()
        arrived(o_copy, j)
        o_own(j).wait()

    statistics.wait()


def local(n, gradients, left_stats, right_stats, left_roots, right_roots, due_factors, block_owner):
    blocks, quarter, extent = gradients.shape
    each = blocks // n
    half = extent // 2
    anywhere = pl.BlockSpec(memory_space=pl.ANY)
    dma = pltpu.SemaphoreType.DMA
    words = due_factors.shape[0], block_owner.shape[0]
    stats, results = pl.pallas_call(
        functools.partial(kernel, n),
        out_shape=(
            jax.ShapeDtypeStruct((2, blocks, quarter, extent), F32),
            jax.ShapeDtypeStruct((3, blocks, quarter, extent), F32),
        ),
        in_specs=[anywhere] * 7,
        out_specs=(anywhere, anywhere),
        scratch_shapes=[
            pltpu.VMEM((1, words[0]), jnp.int32),
            pltpu.VMEM((1, words[1]), jnp.int32),
            pltpu.VMEM((each, extent, extent), F32),
            pltpu.VMEM((2, blocks, quarter, extent), F32),
            pltpu.VMEM((2, blocks, quarter, extent), F32),
            pltpu.VMEM((2, blocks, quarter, extent), F32),
            pltpu.VMEM((blocks, 2, quarter, half), F32),
            pltpu.VMEM((n, each, 2, quarter, half), F32),
            pltpu.VMEM((2, each, extent, extent), F32),
            pltpu.VMEM((2, each, extent, extent), F32),
            pltpu.VMEM((2, blocks, quarter, extent), F32),
            pltpu.VMEM((3, each, extent, extent), F32),
            pltpu.VMEM((2, blocks, half), F32),
            pltpu.VMEM((2, each, quarter, half), F32),
            pltpu.VMEM((2, each, quarter, half), F32),
            pltpu.VMEM((2, each, 2, quarter, half), F32),
            pltpu.VMEM((2, each, 3, quarter, half), F32),
            pltpu.VMEM((2, extent, extent), F32),
            pltpu.VMEM((4, extent, extent), F32),
            pltpu.VMEM((4, extent, extent), F32),
            dma((6,)),
            dma((2,)),
            dma((2, each)),
        ] + [dma((2, 3, each))] * 8,
        compiler_params=pltpu.CompilerParams(
            collective_id=0, has_side_effects=True, vmem_limit_bytes=VMEM_LIMIT
        ),
        cost_estimate=pl.CostEstimate(
            flops=280 * 3 * 2 * extent ** 3, bytes_accessed=10 * 4 * blocks * quarter * extent, transcendentals=0
        ),
    )(
        gradients, left_stats, right_stats, left_roots, right_roots,
        due_factors.reshape(1, -1), block_owner.reshape(1, -1),
    )
    return (stats[0], stats[1], results[0], results[1], results[2])


def solution(mesh):
    spec = P("dp", "shard", None)
    return jax.shard_map(
        functools.partial(local, mesh.shape["shard"]),
        mesh=mesh,
        in_specs=(spec,) * 5 + (P(), P()),
        out_specs=(spec,) * 5,
        check_vma=False,
    )
```

```python
import functools

import jax
import jax.numpy as jnp
from jax import lax
from jax.experimental import pallas as pl
from jax.experimental.pallas import tpu as pltpu
from jax.sharding import PartitionSpec as P

ITERS = 10
STAT_DECAY = 0.95
MESH = pl.DeviceIdType.MESH
VMEM_LIMIT = 63 * 1024 * 1024
F32 = jnp.float32
BF16 = jnp.bfloat16


def split(a):
    high = a.astype(BF16)
    low = (a - high.astype(F32)).astype(BF16)
    return high, low


def dot(a, b):
    return jnp.dot(a, b, preferred_element_type=F32)


def mm(a, b):
    ah, al = a
    bh, bl = b
    rows = ah.shape[0]
    both = dot(jnp.concatenate([ah, al], axis=0), bh)
    return both[:rows] + both[rows:] + dot(ah, bl)


def mirrored(a, b):
    ah, al = a
    rows = ah.shape[0]
    both = dot(jnp.concatenate([ah, al], axis=0), b[0])
    low = both[rows:]
    return both[:rows] + (low + low.T)


def mirrored_and(a, x):
    (ah, al), (xh, xl) = a, x
    rows = ah.shape[0]
    all_four = dot(jnp.concatenate([ah, al, xh, xl], axis=0), ah)
    low = all_four[rows:2 * rows]
    square = all_four[:rows] + (low + low.T)
    product = all_four[2 * rows:3 * rows] + all_four[3 * rows:] + dot(xh, al)
    return square, product


def kernel(
    n,
    g, ls, rs, lr, rr, due, own,
    stats_out, roots_out, update_out,
    duev, ownv, gf, st, rt, sel, spk, pk, p, gg, rg, out, ro, upd, mk,
    fg, fs, fu, gp, gm, gx, rp, rm, rx,
    spread, mat, root,
    load_sem, own_sem, keep_sem,
    g_send, g_recv, s_send, s_recv, q_send, q_recv, r_send, r_recv, u_send, u_recv,
):
    blocks, quarter, extent = g.shape
    each = blocks // n
    half = extent // 2
    me = lax.axis_index("shard")
    group = lax.axis_index("dp")
    right = lax.rem(me + 1, n)
    left = lax.rem(me + n - 1, n)
    opposite = lax.rem(me + 2, n)
    sides = ((right, left), (left, right))

    def rows(index):
        return pl.ds(pl.multiple_of(index * quarter, quarter), quarter)

    def cols(d):
        return pl.ds(d * half, half)

    def remote(src, dst, send, recv, device):
        return pltpu.make_async_remote_copy(
            src_ref=src, dst_ref=dst, send_sem=send, recv_sem=recv,
            device_id=(group, device), device_id_type=MESH,
        )

    def g_copy(d, stage, j):
        device, origin = sides[d]
        return remote(*(
            (g.at[opposite * each + j, :, cols(d)], fg.at[d, j], g_send.at[d, 0, j], g_recv.at[d, 0, j], device),
            (g.at[device * each + j], gf.at[j, rows(me), :], g_send.at[d, 1, j], g_recv.at[d, 1, j], device),
            (fg.at[d, j], gf.at[j, rows(origin), cols(d)], g_send.at[d, 2, j], g_recv.at[d, 2, j], device),
        )[stage])

    def s_copy(d, stage, j):
        device, origin = sides[d]
        return remote(*(
            (spk.at[opposite * each + j, d], fs.at[d, j], s_send.at[d, 0, j], s_recv.at[d, 0, j], device),
            (spk.at[device * each + j], pk.at[me, j], s_send.at[d, 1, j], s_recv.at[d, 1, j], device),
            (fs.at[d, j], pk.at[origin, j, d], s_send.at[d, 2, j], s_recv.at[d, 2, j], device),
        )[stage])

    def u_copy(d, stage, j):
        device, origin = sides[d]
        return remote(*(
            (upd.at[j, rows(opposite), cols(d)], fu.at[d, j], u_send.at[d, 0, j], u_recv.at[d, 0, j], device),
            (upd.at[j, rows(device), :], update_out.at[me * each + j], u_send.at[d, 1, j], u_recv.at[d, 1, j], device),
            (fu.at[d, j], update_out.at[origin * each + j, :, cols(d)], u_send.at[d, 2, j], u_recv.at[d, 2, j], device),
        )[stage])

    low_lanes = lax.broadcasted_iota(jnp.int32, (quarter, half), 1) < quarter

    def place(value, parity, to):
        return jnp.where(parity == to, value, pltpu.roll(value, quarter, 1))

    def pick(first, second, index, to):
        return place(jnp.where(index // 2 == 0, first, second), lax.rem(index, 2), to)

    class Mirrored:
        def __init__(self, src, dst, packed, passing, landed, send, recv):
            self.src, self.dst, self.packed = src, dst, packed
            self.passing, self.landed, self.send, self.recv = passing, landed, send, recv

        def copy(self, d, stage, j):
            device, origin = sides[d]
            src, dst = (
                (self.packed.at[d, j], self.passing.at[d, j, 0]),
                (self.src.at[:, j, rows(device), :], self.dst.at[:, me * each + j]),
                (self.passing.at[d, j], self.landed.at[d, j]),
            )[stage]
            return remote(src, dst, self.send.at[d, stage, j], self.recv.at[d, stage, j], device)

        def begin(self, j):
            parts = [
                [self.src[i, j, rows(opposite), e * half:(e + 1) * half] for e in (0, 1)]
                for i in (0, 1)
            ]
            for d, index in ((0, me), (1, opposite)):
                self.packed[d, j] = jnp.where(
                    low_lanes, pick(*parts[0], index, 0), pick(*parts[1], index, 1)
                )
            begin(self.copy, j)

        def forward(self, j):
            for d in (0, 1):
                device, origin = sides[d]
                self.copy(d, 0, j).wait_recv()
                self.copy(d, 1, j).wait_recv()
                parts = [
                    pick(
                        self.dst[i, origin * each + j, :, 0:half],
                        self.dst[i, origin * each + j, :, half:extent],
                        device, 0,
                    )
                    for i in (1, 0)
                ]
                self.passing[d, j, 1] = jnp.concatenate(parts, axis=0).T[0:quarter, :]
                self.copy(d, 2, j).start()

        def assemble(self, j):
            for d in (0, 1):
                self.copy(d, 2, j).wait_recv()
            pieces = (
                (self.landed[0, j, 0], opposite, 0),
                (self.landed[0, j, 1], left, 1),
                (self.landed[1, j, 0], me, 0),
                (self.landed[1, j, 1], right, 1),
            )
            for i in (0, 1):
                placed = [
                    (index, place(piece, lax.rem(index, 2), (where + i) % 2))
                    for piece, index, where in pieces
                ]
                for e in (0, 1):
                    part = 2 * e + jnp.where(low_lanes, 0, 1)
                    value = placed[0][1]
                    for index, piece in placed[1:]:
                        value = jnp.where(part == index, piece, value)
                    self.dst[i, opposite * each + j, :, e * half:(e + 1) * half] = value

        def sent(self, j):
            for d in (0, 1):
                for stage in (0, 1, 2):
                    self.copy(d, stage, j).wait_send()

    def begin(copy, j):
        for stage in (0, 1):
            for d in (0, 1):
                copy(d, stage, j).start()

    def forward(copy, j):
        for d in (0, 1):
            copy(d, 0, j).wait_recv()
            copy(d, 2, j).start()

    def arrived(copy, j):
        for d in (0, 1):
            for stage in (1, 2):
                copy(d, stage, j).wait_recv()

    grams = Mirrored(gg, rg, gp, gm, gx, q_send, q_recv)
    results = Mirrored(out, ro, rp, rm, rx, r_send, r_recv)

    def q_own(j):
        return pltpu.make_async_copy(
            gg.at[:, j, rows(me), :], rg.at[:, me * each + j], own_sem.at[1, j]
        )

    def r_own(j):
        return pltpu.make_async_copy(
            out.at[:, j, rows(me), :], roots_out.at[:, me * each + j], own_sem.at[2, j]
        )

    def u_own(j):
        return pltpu.make_async_copy(
            upd.at[j, rows(me), :], update_out.at[me * each + j], own_sem.at[3, j]
        )

    def keep(owner, j, slot):
        return pltpu.make_async_copy(
            ro.at[:, owner * each + j], roots_out.at[:, owner * each + j], keep_sem.at[slot, j]
        )

    def returned(j):
        results.assemble(j)
        for slot, owner in enumerate((left, right, opposite)):
            keep(owner, j, slot).start()

    def statistics_copy():
        return pltpu.make_async_copy(rg, stats_out, own_sem.at[0, 1])

    def statistics():
        @pl.loop(0, each)
        def _(j):
            q_own(j).wait()
            grams.assemble(j)

        @pl.loop(0, blocks)
        def _(b):
            for side in (0, 1):
                rg[side, b] = STAT_DECAY * st[side, b] + (1.0 - STAT_DECAY) * rg[side, b]

        statistics_copy().start()

    loads = [
        pltpu.make_async_copy(ref, place, load_sem.at[i])
        for i, (ref, place) in enumerate(
            ((due, duev), (own, ownv), (ls, st.at[0]), (rs, st.at[1]), (lr, rt.at[0]), (rr, rt.at[1]))
        )
    ]
    own_rows = pltpu.make_async_copy(
        g.at[pl.ds(me * each, each)], gf.at[:, rows(me), :], own_sem.at[0, 0]
    )
    for load in loads:
        load.start()

    barrier = pltpu.get_barrier_semaphore()
    for device in (left, right):
        pl.semaphore_signal(barrier, inc=1, device_id=(group, device), device_id_type=MESH)
    pl.semaphore_wait(barrier, 2)

    begin(g_copy, 0)
    own_rows.start()

    total = own.shape[1]
    for load in loads[:2]:
        load.wait()
    slots = group * blocks + lax.broadcasted_iota(jnp.int32, (blocks, total), 0)
    numbers = lax.broadcasted_iota(jnp.int32, (blocks, total), 1)
    stored = jnp.where(ownv[...] == slots, numbers, 0).astype(F32)
    number = jnp.sum(stored, axis=1, keepdims=True)
    entries = duev[...].astype(F32)
    for side in (0, 1):
        hit = jnp.where(entries == 2.0 * number + side, 1.0, 0.0)
        flag = jnp.max(hit, axis=1, keepdims=True)
        mk[side] = jnp.broadcast_to(flag, (blocks, half))

    for load in loads[2:]:
        load.wait()

    def choose(j, owner):
        b = owner * each + j
        second = lax.rem(jnp.where(owner == right, me + 2, me + 1), n)
        for side in (0, 1):
            flag = mk[side, pl.ds(b, 1), :] > 0.5
            halves = []
            for d in (0, 1):
                value = jnp.where(
                    flag,
                    st[side, b, :, d * half:(d + 1) * half],
                    rt[side, b, :, d * half:(d + 1) * half],
                )
                sel[side, b, :, d * half:(d + 1) * half] = value
                halves.append(value)
            spk[b, side] = jnp.where(
                low_lanes, pick(*halves, me, 0), pick(*halves, second, 1)
            )

    def choose_all(j):
        @pl.loop(0, n)
        def _(owner):
            choose(j, owner)

    choose_all(0)
    begin(s_copy, 0)
    begin(g_copy, 1)
    for j in range(1, each):
        choose_all(j)
    forward(g_copy, 0)
    forward(s_copy, 0)
    begin(s_copy, 1)
    begin(g_copy, 2)
    begin(s_copy, 2)
    forward(g_copy, 1)
    own_rows.wait()

    row_ids = lax.broadcasted_iota(jnp.int32, (extent, extent), 0)
    col_ids = lax.broadcasted_iota(jnp.int32, (extent, extent), 1)
    diagonal = row_ids == col_ids
    mat[...] = jnp.zeros_like(mat)
    root[...] = jnp.zeros_like(root)

    def partner(row):
        return lax.rem(row + jnp.where(row == left, 2, 1), n)

    def gram(j):
        arrived(g_copy, j)
        grad = gf[j]
        straight, turned = split(grad), split(grad.T)
        gg[0, j] = mirrored(straight, turned)
        gg[1, j] = mirrored(turned, straight)
        grams.begin(j)
        q_own(j).start()

    def prepare(j, chain):
        arrived(s_copy, j)
        row_part, col_part = row_ids // quarter, col_ids // quarter
        other = lax.rem(row_part + jnp.where(row_part == left, 2, 1), n)
        known = (row_part == me) | (row_part == col_part) | (col_part == other)
        for i in (0, 1):
            for row in range(n):
                second = partner(row)
                packed = pk[row, j, i]
                turned_round = pltpu.roll(packed, quarter, 1)
                low = packed if row % 2 == 0 else turned_round
                high = jnp.where(lax.rem(second, 2) == 1, packed, turned_round)
                for d in (0, 1):
                    part = 2 * d + jnp.where(low_lanes, 0, 1)
                    value = jnp.where(part == row, low, jnp.where(part == second, high, 0.0))
                    value = jnp.where(
                        me == row, sel[i, me * each + j, :, d * half:(d + 1) * half], value
                    )
                    spread[i, row * quarter:(row + 1) * quarter, d * half:(d + 1) * half] = value
            whole = spread[i]
            whole = jnp.where(known, whole, whole.T)
            p[i, j] = whole
            chosen = STAT_DECAY * whole + (1.0 - STAT_DECAY) * gg[i, j]
            frobenius = jnp.sqrt(jnp.sum(chosen * chosen, keepdims=True))
            mat[chain + i] = chosen / frobenius
            root[chain + i] = jnp.where(diagonal, 1.0 / jnp.sqrt(jnp.sqrt(frobenius)), 0.0)

    def finish(j, chain):
        for i in (0, 1):
            flag = mk[i, pl.ds(me * each + j, 1), :] > 0.5
            for d in (0, 1):
                out[i, j, :, d * half:(d + 1) * half] = jnp.where(
                    flag,
                    root[chain + i, :, d * half:(d + 1) * half],
                    p[i, j, :, d * half:(d + 1) * half],
                )
        results.begin(j)
        r_own(j).start()
        middle = mm(split(out[0, j]), split(gf[j]))
        upd[j] = mm(split(middle), split(out[1, j]))
        begin(u_copy, j)
        u_own(j).start()

    gram(0)
    prepare(0, 0)
    forward(s_copy, 1)
    begin(g_copy, 3)
    begin(s_copy, 3)

    def body():
        chains = range(4)
        factor = [jnp.where(diagonal, 1.25, 0.0) - 0.25 * mat[i] for i in chains]
        parts = [split(f) for f in factor]
        square = [mirrored(f, f) for f in parts]
        parts = [split(f) for f in square]
        fourth = [mirrored(f, f) for f in parts]
        term = [
            mm(split(q), split(5.0 * f - 4.0 * s))
            for q, f, s in zip(fourth, factor, square)
        ]
        joint = [split(1.25 * f - 0.25 * u) for f, u in zip(factor, term)]
        both = [mirrored_and(joint[i], split(root[i])) for i in chains]
        parts = [split(square) for square, _ in both]
        fourth = [mirrored(f, f) for f in parts]
        matrix = [mm(split(fourth[i]), split(mat[i])) for i in chains]
        for i in chains:
            root[i] = both[i][1]
            mat[i] = matrix[i]

    pairs = ITERS // 2

    @pl.loop(0, 2 * pairs + 1)
    def _(t):
        body()

        def at(step, *actions):
            @pl.when(t == step)
            def _():
                for action, *rest in actions:
                    action(*rest)

        @pl.when(t < pairs - 1)
        def _():
            at(0, (forward, g_copy, 2), (forward, s_copy, 2), (gram, 1), (prepare, 1, 2))
            at(1, (forward, g_copy, 3), (forward, s_copy, 3), (gram, 2))
            at(2, (grams.forward, 0), (gram, 3))
            at(3, (grams.forward, 1))

        @pl.when(t >= pairs - 1)
        def _():
            @pl.when(lax.rem(t, pairs) == pairs - 1)
            def _():
                finish(2 * (t // pairs), 0)

            @pl.when(lax.rem(t, pairs) == 0)
            def _():
                finish(2 * (t // pairs) - 1, 2)

            at(pairs - 1, (prepare, 2, 0))
            at(pairs, (prepare, 3, 2), (grams.forward, 2))
            at(6, (grams.forward, 3))
            at(7, (results.forward, 0), (forward, u_copy, 0))
            at(8, (results.forward, 1), (forward, u_copy, 1))

    for j in (2, 3):
        results.forward(j)
        forward(u_copy, j)

    statistics()

    @pl.loop(0, each)
    def _(j):
        returned(j)

    @pl.loop(0, each)
    def _(j):
        for copy in (g_copy, s_copy, u_copy):
            for d in (0, 1):
                for stage in (0, 1, 2):
                    copy(d, stage, j).wait_send()
        grams.sent(j)
        results.sent(j)
        arrived(u_copy, j)
        r_own(j).wait()
        u_own(j).wait()
        for slot, owner in enumerate((left, right, opposite)):
            keep(owner, j, slot).wait()

    statistics_copy().wait()


def local(n, gradients, left_stats, right_stats, left_roots, right_roots, due_factors, block_owner):
    blocks, quarter, extent = gradients.shape
    each = blocks // n
    half = extent // 2
    anywhere = pl.BlockSpec(memory_space=pl.ANY)
    dma = pltpu.SemaphoreType.DMA
    words = due_factors.shape[0], block_owner.shape[0]
    stats, roots, update = pl.pallas_call(
        functools.partial(kernel, n),
        out_shape=(
            jax.ShapeDtypeStruct((2, blocks, quarter, extent), F32),
            jax.ShapeDtypeStruct((2, blocks, quarter, extent), F32),
            jax.ShapeDtypeStruct((blocks, quarter, extent), F32),
        ),
        in_specs=[anywhere] * 7,
        out_specs=(anywhere,) * 3,
        scratch_shapes=[
            pltpu.VMEM((1, words[0]), jnp.int32),
            pltpu.VMEM((1, words[1]), jnp.int32),
            pltpu.VMEM((each, extent, extent), F32),
            pltpu.VMEM((2, blocks, quarter, extent), F32),
            pltpu.VMEM((2, blocks, quarter, extent), F32),
            pltpu.VMEM((2, blocks, quarter, extent), F32),
            pltpu.VMEM((blocks, 2, quarter, half), F32),
            pltpu.VMEM((n, each, 2, quarter, half), F32),
            pltpu.VMEM((2, each, extent, extent), F32),
            pltpu.VMEM((2, each, extent, extent), F32),
            pltpu.VMEM((2, blocks, quarter, extent), F32),
            pltpu.VMEM((2, each, extent, extent), F32),
            pltpu.VMEM((2, blocks, quarter, extent), F32),
            pltpu.VMEM((each, extent, extent), F32),
            pltpu.VMEM((2, blocks, half), F32),
            pltpu.VMEM((2, each, quarter, half), F32),
            pltpu.VMEM((2, each, quarter, half), F32),
            pltpu.VMEM((2, each, quarter, half), F32),
        ] + [
            pltpu.VMEM((2, each, quarter, half), F32),
            pltpu.VMEM((2, each, 2, quarter, half), F32),
            pltpu.VMEM((2, each, 2, quarter, half), F32),
        ] * 2 + [
            pltpu.VMEM((2, extent, extent), F32),
            pltpu.VMEM((4, extent, extent), F32),
            pltpu.VMEM((4, extent, extent), F32),
            dma((6,)),
            dma((4, each)),
            dma((3, each)),
        ] + [dma((2, 3, each))] * 10,
        compiler_params=pltpu.CompilerParams(
            collective_id=0, has_side_effects=True, vmem_limit_bytes=VMEM_LIMIT
        ),
        cost_estimate=pl.CostEstimate(
            flops=280 * 3 * 2 * extent ** 3, bytes_accessed=10 * 4 * blocks * quarter * extent, transcendentals=0
        ),
    )(
        gradients, left_stats, right_stats, left_roots, right_roots,
        due_factors.reshape(1, -1), block_owner.reshape(1, -1),
    )
    return (stats[0], stats[1], roots[0], roots[1], update)


def solution(mesh):
    spec = P("dp", "shard", None)
    return jax.shard_map(
        functools.partial(local, mesh.shape["shard"]),
        mesh=mesh,
        in_specs=(spec,) * 5 + (P(), P()),
        out_specs=(spec,) * 5,
        check_vma=False,
    )
```

```python
import functools

import jax
import jax.numpy as jnp
from jax import lax
from jax.experimental import pallas as pl
from jax.experimental.pallas import tpu as pltpu
from jax.sharding import PartitionSpec as P

ITERS = 10
STAT_DECAY = 0.95
MESH = pl.DeviceIdType.MESH
VMEM_LIMIT = 63 * 1024 * 1024
F32 = jnp.float32
BF16 = jnp.bfloat16


def split(a):
    high = a.astype(BF16)
    low = (a - high.astype(F32)).astype(BF16)
    return high, low


def mm(a, b):
    ah, al = a
    bh, bl = b
    return jnp.dot(
        jnp.concatenate([ah, ah, al], axis=1),
        jnp.concatenate([bh, bl, bh], axis=0),
        preferred_element_type=F32,
    )


def kernel(
    n,
    g, ls, rs, lr, rr, due, own,
    stats_out, roots_out, update_out,
    duev, ownv, gf, st, rt, sel, spk, pk, p, gg, rg, out, ro, upd, mk,
    fg, fs, fu, gp, gm, gx, rp, rm, rx,
    spread, mat, root,
    load_sem, own_sem, keep_sem,
    g_send, g_recv, s_send, s_recv, q_send, q_recv, r_send, r_recv, u_send, u_recv,
):
    blocks, quarter, extent = g.shape
    each = blocks // n
    half = extent // 2
    me = lax.axis_index("shard")
    group = lax.axis_index("dp")
    right = lax.rem(me + 1, n)
    left = lax.rem(me + n - 1, n)
    opposite = lax.rem(me + 2, n)
    sides = ((right, left), (left, right))

    def rows(index):
        return pl.ds(pl.multiple_of(index * quarter, quarter), quarter)

    def cols(d):
        return pl.ds(d * half, half)

    def remote(src, dst, send, recv, device):
        return pltpu.make_async_remote_copy(
            src_ref=src, dst_ref=dst, send_sem=send, recv_sem=recv,
            device_id=(group, device), device_id_type=MESH,
        )

    def g_copy(d, stage, j):
        device, origin = sides[d]
        return remote(*(
            (g.at[opposite * each + j, :, cols(d)], fg.at[d, j], g_send.at[d, 0, j], g_recv.at[d, 0, j], device),
            (g.at[device * each + j], gf.at[j, rows(me), :], g_send.at[d, 1, j], g_recv.at[d, 1, j], device),
            (fg.at[d, j], gf.at[j, rows(origin), cols(d)], g_send.at[d, 2, j], g_recv.at[d, 2, j], device),
        )[stage])

    def s_copy(d, stage, j):
        device, origin = sides[d]
        return remote(*(
            (spk.at[opposite * each + j, d], fs.at[d, j], s_send.at[d, 0, j], s_recv.at[d, 0, j], device),
            (spk.at[device * each + j], pk.at[me, j], s_send.at[d, 1, j], s_recv.at[d, 1, j], device),
            (fs.at[d, j], pk.at[origin, j, d], s_send.at[d, 2, j], s_recv.at[d, 2, j], device),
        )[stage])

    def u_copy(d, stage, j):
        device, origin = sides[d]
        return remote(*(
            (upd.at[j, rows(opposite), cols(d)], fu.at[d, j], u_send.at[d, 0, j], u_recv.at[d, 0, j], device),
            (upd.at[j, rows(device), :], update_out.at[me * each + j], u_send.at[d, 1, j], u_recv.at[d, 1, j], device),
            (fu.at[d, j], update_out.at[origin * each + j, :, cols(d)], u_send.at[d, 2, j], u_recv.at[d, 2, j], device),
        )[stage])

    low_lanes = lax.broadcasted_iota(jnp.int32, (quarter, half), 1) < quarter

    def place(value, parity, to):
        return jnp.where(parity == to, value, pltpu.roll(value, quarter, 1))

    def pick(first, second, index, to):
        return place(jnp.where(index // 2 == 0, first, second), lax.rem(index, 2), to)

    class Mirrored:
        def __init__(self, src, dst, packed, passing, landed, send, recv):
            self.src, self.dst, self.packed = src, dst, packed
            self.passing, self.landed, self.send, self.recv = passing, landed, send, recv

        def copy(self, d, stage, j):
            device, origin = sides[d]
            src, dst = (
                (self.packed.at[d, j], self.passing.at[d, j, 0]),
                (self.src.at[:, j, rows(device), :], self.dst.at[:, me * each + j]),
                (self.passing.at[d, j], self.landed.at[d, j]),
            )[stage]
            return remote(src, dst, self.send.at[d, stage, j], self.recv.at[d, stage, j], device)

        def begin(self, j):
            parts = [
                [self.src[i, j, rows(opposite), e * half:(e + 1) * half] for e in (0, 1)]
                for i in (0, 1)
            ]
            for d, index in ((0, me), (1, opposite)):
                self.packed[d, j] = jnp.where(
                    low_lanes, pick(*parts[0], index, 0), pick(*parts[1], index, 1)
                )
            begin(self.copy, j)

        def forward(self, j):
            for d in (0, 1):
                device, origin = sides[d]
                self.copy(d, 0, j).wait_recv()
                self.copy(d, 1, j).wait_recv()
                parts = [
                    pick(
                        self.dst[i, origin * each + j, :, 0:half],
                        self.dst[i, origin * each + j, :, half:extent],
                        device, 0,
                    )
                    for i in (1, 0)
                ]
                self.passing[d, j, 1] = jnp.concatenate(parts, axis=0).T[0:quarter, :]
                self.copy(d, 2, j).start()

        def assemble(self, j):
            for d in (0, 1):
                self.copy(d, 2, j).wait_recv()
            pieces = (
                (self.landed[0, j, 0], opposite, 0),
                (self.landed[0, j, 1], left, 1),
                (self.landed[1, j, 0], me, 0),
                (self.landed[1, j, 1], right, 1),
            )
            for i in (0, 1):
                placed = [
                    (index, place(piece, lax.rem(index, 2), (where + i) % 2))
                    for piece, index, where in pieces
                ]
                for e in (0, 1):
                    part = 2 * e + jnp.where(low_lanes, 0, 1)
                    value = placed[0][1]
                    for index, piece in placed[1:]:
                        value = jnp.where(part == index, piece, value)
                    self.dst[i, opposite * each + j, :, e * half:(e + 1) * half] = value

        def sent(self, j):
            for d in (0, 1):
                for stage in (0, 1, 2):
                    self.copy(d, stage, j).wait_send()

    def begin(copy, j):
        for stage in (0, 1):
            for d in (0, 1):
                copy(d, stage, j).start()

    def forward(copy, j):
        for d in (0, 1):
            copy(d, 0, j).wait_recv()
            copy(d, 2, j).start()

    def arrived(copy, j):
        for d in (0, 1):
            for stage in (1, 2):
                copy(d, stage, j).wait_recv()

    grams = Mirrored(gg, rg, gp, gm, gx, q_send, q_recv)
    results = Mirrored(out, ro, rp, rm, rx, r_send, r_recv)

    def q_own(j):
        return pltpu.make_async_copy(
            gg.at[:, j, rows(me), :], rg.at[:, me * each + j], own_sem.at[1, j]
        )

    def r_own(j):
        return pltpu.make_async_copy(
            out.at[:, j, rows(me), :], roots_out.at[:, me * each + j], own_sem.at[2, j]
        )

    def u_own(j):
        return pltpu.make_async_copy(
            upd.at[j, rows(me), :], update_out.at[me * each + j], own_sem.at[3, j]
        )

    def keep(owner, j, slot):
        return pltpu.make_async_copy(
            ro.at[:, owner * each + j], roots_out.at[:, owner * each + j], keep_sem.at[slot, j]
        )

    def returned(j):
        results.assemble(j)
        for slot, owner in enumerate((left, right, opposite)):
            keep(owner, j, slot).start()

    def statistics_copy():
        return pltpu.make_async_copy(rg, stats_out, own_sem.at[0, 1])

    def statistics():
        @pl.loop(0, each)
        def _(j):
            q_own(j).wait()
            grams.assemble(j)

        @pl.loop(0, blocks)
        def _(b):
            for side in (0, 1):
                rg[side, b] = STAT_DECAY * st[side, b] + (1.0 - STAT_DECAY) * rg[side, b]

        statistics_copy().start()

    loads = [
        pltpu.make_async_copy(ref, place, load_sem.at[i])
        for i, (ref, place) in enumerate(
            ((due, duev), (own, ownv), (ls, st.at[0]), (rs, st.at[1]), (lr, rt.at[0]), (rr, rt.at[1]))
        )
    ]
    own_rows = pltpu.make_async_copy(
        g.at[pl.ds(me * each, each)], gf.at[:, rows(me), :], own_sem.at[0, 0]
    )
    for load in loads:
        load.start()

    barrier = pltpu.get_barrier_semaphore()
    for device in (left, right):
        pl.semaphore_signal(barrier, inc=1, device_id=(group, device), device_id_type=MESH)
    pl.semaphore_wait(barrier, 2)

    begin(g_copy, 0)
    own_rows.start()

    total = own.shape[1]
    for load in loads[:2]:
        load.wait()
    slots = group * blocks + lax.broadcasted_iota(jnp.int32, (blocks, total), 0)
    numbers = lax.broadcasted_iota(jnp.int32, (blocks, total), 1)
    stored = jnp.where(ownv[...] == slots, numbers, 0).astype(F32)
    number = jnp.sum(stored, axis=1, keepdims=True)
    entries = duev[...].astype(F32)
    for side in (0, 1):
        hit = jnp.where(entries == 2.0 * number + side, 1.0, 0.0)
        flag = jnp.max(hit, axis=1, keepdims=True)
        mk[side] = jnp.broadcast_to(flag, (blocks, half))

    for load in loads[2:]:
        load.wait()

    def choose(j, owner):
        b = owner * each + j
        second = lax.rem(jnp.where(owner == right, me + 2, me + 1), n)
        for side in (0, 1):
            flag = mk[side, pl.ds(b, 1), :] > 0.5
            halves = []
            for d in (0, 1):
                value = jnp.where(
                    flag,
                    st[side, b, :, d * half:(d + 1) * half],
                    rt[side, b, :, d * half:(d + 1) * half],
                )
                sel[side, b, :, d * half:(d + 1) * half] = value
                halves.append(value)
            spk[b, side] = jnp.where(
                low_lanes, pick(*halves, me, 0), pick(*halves, second, 1)
            )

    def choose_all(j):
        @pl.loop(0, n)
        def _(owner):
            choose(j, owner)

    choose_all(0)
    begin(s_copy, 0)
    begin(g_copy, 1)
    choose_all(1)
    forward(g_copy, 0)
    forward(s_copy, 0)
    begin(s_copy, 1)
    for j in range(2, each):
        choose_all(j)
    forward(g_copy, 1)
    forward(s_copy, 1)
    begin(g_copy, 2)
    begin(s_copy, 2)
    own_rows.wait()

    row_ids = lax.broadcasted_iota(jnp.int32, (extent, extent), 0)
    col_ids = lax.broadcasted_iota(jnp.int32, (extent, extent), 1)
    diagonal = row_ids == col_ids
    mat[...] = jnp.zeros_like(mat)
    root[...] = jnp.zeros_like(root)

    def partner(row):
        return lax.rem(row + jnp.where(row == left, 2, 1), n)

    def gram(j):
        arrived(g_copy, j)
        grad = gf[j]
        straight, turned = split(grad), split(grad.T)
        gg[0, j] = mm(straight, turned)
        gg[1, j] = mm(turned, straight)
        grams.begin(j)
        q_own(j).start()

    def prepare(j, chain):
        arrived(s_copy, j)
        row_part, col_part = row_ids // quarter, col_ids // quarter
        other = lax.rem(row_part + jnp.where(row_part == left, 2, 1), n)
        known = (row_part == me) | (row_part == col_part) | (col_part == other)
        for i in (0, 1):
            for row in range(n):
                second = partner(row)
                packed = pk[row, j, i]
                turned_round = pltpu.roll(packed, quarter, 1)
                low = packed if row % 2 == 0 else turned_round
                high = jnp.where(lax.rem(second, 2) == 1, packed, turned_round)
                for d in (0, 1):
                    part = 2 * d + jnp.where(low_lanes, 0, 1)
                    value = jnp.where(part == row, low, jnp.where(part == second, high, 0.0))
                    value = jnp.where(
                        me == row, sel[i, me * each + j, :, d * half:(d + 1) * half], value
                    )
                    spread[i, row * quarter:(row + 1) * quarter, d * half:(d + 1) * half] = value
            whole = spread[i]
            whole = jnp.where(known, whole, whole.T)
            p[i, j] = whole
            chosen = STAT_DECAY * whole + (1.0 - STAT_DECAY) * gg[i, j]
            frobenius = jnp.sqrt(jnp.sum(chosen * chosen, keepdims=True))
            mat[chain + i] = chosen / frobenius
            root[chain + i] = jnp.where(diagonal, 1.0 / jnp.sqrt(jnp.sqrt(frobenius)), 0.0)

    def finish(j, chain):
        for i in (0, 1):
            flag = mk[i, pl.ds(me * each + j, 1), :] > 0.5
            for d in (0, 1):
                out[i, j, :, d * half:(d + 1) * half] = jnp.where(
                    flag,
                    root[chain + i, :, d * half:(d + 1) * half],
                    p[i, j, :, d * half:(d + 1) * half],
                )
        results.begin(j)
        r_own(j).start()
        middle = mm(split(out[0, j]), split(gf[j]))
        upd[j] = mm(split(middle), split(out[1, j]))
        begin(u_copy, j)
        u_own(j).start()

    gram(0)
    prepare(0, 0)
    begin(g_copy, 3)
    begin(s_copy, 3)

    def steps(i):
        factor = jnp.where(diagonal, 1.25, 0.0) - 0.25 * mat[i]
        parts = split(factor)
        yield
        square = mm(parts, parts)
        yield
        parts = split(square)
        rest = split(5.0 * factor - 4.0 * square)
        yield
        fourth = mm(parts, parts)
        yield
        parts = split(fourth)
        yield
        term = mm(parts, rest)
        yield
        joint = split(1.25 * factor - 0.25 * term)
        yield
        square = mm(joint, joint)
        yield
        parts = split(square)
        before = split(root[i])
        yield
        fourth = mm(parts, parts)
        root[i] = mm(before, joint)
        yield
        parts = split(fourth)
        rest = split(mat[i])
        yield
        matrix = mm(parts, rest)
        yield
        mat[i] = matrix
        yield

    def body():
        chains = [steps(i) for i in range(4)]
        waiting = None
        for stage in range(6):
            for chain in chains:
                if stage == 0:
                    next(chain)
                next(chain)
                if waiting is not None:
                    next(waiting)
                waiting = chain
        next(waiting)

    pairs = ITERS // 2

    @pl.loop(0, 2 * pairs + 1)
    def _(t):
        body()

        def at(step, *actions):
            @pl.when(t == step)
            def _():
                for action, *rest in actions:
                    action(*rest)

        @pl.when(t < pairs - 1)
        def _():
            at(0, (forward, g_copy, 2), (forward, s_copy, 2), (gram, 1), (prepare, 1, 2))
            at(1, (forward, g_copy, 3), (forward, s_copy, 3), (gram, 2))
            at(2, (grams.forward, 0), (gram, 3))
            at(3, (grams.forward, 1))

        @pl.when(t >= pairs - 1)
        def _():
            @pl.when(lax.rem(t, pairs) == pairs - 1)
            def _():
                finish(2 * (t // pairs), 0)

            @pl.when(lax.rem(t, pairs) == 0)
            def _():
                finish(2 * (t // pairs) - 1, 2)

            at(pairs - 1, (prepare, 2, 0))
            at(pairs, (prepare, 3, 2), (grams.forward, 2))
            at(6, (grams.forward, 3))
            at(7, (results.forward, 0), (forward, u_copy, 0))
            at(8, (results.forward, 1), (forward, u_copy, 1))

    for j in (2, 3):
        results.forward(j)
        forward(u_copy, j)

    statistics()

    @pl.loop(0, each)
    def _(j):
        returned(j)

    @pl.loop(0, each)
    def _(j):
        for copy in (g_copy, s_copy, u_copy):
            for d in (0, 1):
                for stage in (0, 1, 2):
                    copy(d, stage, j).wait_send()
        grams.sent(j)
        results.sent(j)
        arrived(u_copy, j)
        r_own(j).wait()
        u_own(j).wait()
        for slot, owner in enumerate((left, right, opposite)):
            keep(owner, j, slot).wait()

    statistics_copy().wait()


def local(n, gradients, left_stats, right_stats, left_roots, right_roots, due_factors, block_owner):
    blocks, quarter, extent = gradients.shape
    each = blocks // n
    half = extent // 2
    anywhere = pl.BlockSpec(memory_space=pl.ANY)
    dma = pltpu.SemaphoreType.DMA
    words = due_factors.shape[0], block_owner.shape[0]
    stats, roots, update = pl.pallas_call(
        functools.partial(kernel, n),
        out_shape=(
            jax.ShapeDtypeStruct((2, blocks, quarter, extent), F32),
            jax.ShapeDtypeStruct((2, blocks, quarter, extent), F32),
            jax.ShapeDtypeStruct((blocks, quarter, extent), F32),
        ),
        in_specs=[anywhere] * 7,
        out_specs=(anywhere,) * 3,
        scratch_shapes=[
            pltpu.VMEM((1, words[0]), jnp.int32),
            pltpu.VMEM((1, words[1]), jnp.int32),
            pltpu.VMEM((each, extent, extent), F32),
            pltpu.VMEM((2, blocks, quarter, extent), F32),
            pltpu.VMEM((2, blocks, quarter, extent), F32),
            pltpu.VMEM((2, blocks, quarter, extent), F32),
            pltpu.VMEM((blocks, 2, quarter, half), F32),
            pltpu.VMEM((n, each, 2, quarter, half), F32),
            pltpu.VMEM((2, each, extent, extent), F32),
            pltpu.VMEM((2, each, extent, extent), F32),
            pltpu.VMEM((2, blocks, quarter, extent), F32),
            pltpu.VMEM((2, each, extent, extent), F32),
            pltpu.VMEM((2, blocks, quarter, extent), F32),
            pltpu.VMEM((each, extent, extent), F32),
            pltpu.VMEM((2, blocks, half), F32),
            pltpu.VMEM((2, each, quarter, half), F32),
            pltpu.VMEM((2, each, quarter, half), F32),
            pltpu.VMEM((2, each, quarter, half), F32),
        ] + [
            pltpu.VMEM((2, each, quarter, half), F32),
            pltpu.VMEM((2, each, 2, quarter, half), F32),
            pltpu.VMEM((2, each, 2, quarter, half), F32),
        ] * 2 + [
            pltpu.VMEM((2, extent, extent), F32),
            pltpu.VMEM((4, extent, extent), F32),
            pltpu.VMEM((4, extent, extent), F32),
            dma((6,)),
            dma((4, each)),
            dma((3, each)),
        ] + [dma((2, 3, each))] * 10,
        compiler_params=pltpu.CompilerParams(
            collective_id=0, has_side_effects=True, vmem_limit_bytes=VMEM_LIMIT
        ),
        cost_estimate=pl.CostEstimate(
            flops=280 * 3 * 2 * extent ** 3, bytes_accessed=10 * 4 * blocks * quarter * extent, transcendentals=0
        ),
    )(
        gradients, left_stats, right_stats, left_roots, right_roots,
        due_factors.reshape(1, -1), block_owner.reshape(1, -1),
    )
    return (stats[0], stats[1], roots[0], roots[1], update)


def solution(mesh):
    spec = P("dp", "shard", None)
    return jax.shard_map(
        functools.partial(local, mesh.shape["shard"]),
        mesh=mesh,
        in_specs=(spec,) * 5 + (P(), P()),
        out_specs=(spec,) * 5,
        check_vma=False,
    )
```

```python
import functools

import jax
import jax.numpy as jnp
from jax import lax
from jax.experimental import pallas as pl
from jax.experimental.pallas import tpu as pltpu
from jax.sharding import PartitionSpec as P

ITERS = 10
STAT_DECAY = 0.95
MESH = pl.DeviceIdType.MESH
VMEM_LIMIT = 63 * 1024 * 1024
F32 = jnp.float32
BF16 = jnp.bfloat16


def split(a):
    high = a.astype(BF16)
    low = (a - high.astype(F32)).astype(BF16)
    return high, low


def mm(a, b):
    ah, al = a
    bh, bl = b
    return jnp.dot(
        jnp.concatenate([ah, ah, al], axis=1),
        jnp.concatenate([bh, bl, bh], axis=0),
        preferred_element_type=F32,
    )


def kernel(
    n,
    g, ls, rs, lr, rr, due, own,
    stats_out, roots_out, update_out,
    duev, ownv, gf, st, rt, sel, spk, pk, p, gg, rg, out, ro, upd, mk,
    fg, fs, fu, gown, gp, gd, ga, gm, gx, rp, rm, rx,
    spread, mat, root,
    load_sem, own_sem, keep_sem,
    g_send, g_recv, s_send, s_recv, q_send, q_recv, r_send, r_recv, u_send, u_recv,
):
    blocks, quarter, extent = g.shape
    each = blocks // n
    half = extent // 2
    me = lax.axis_index("shard")
    group = lax.axis_index("dp")
    right = lax.rem(me + 1, n)
    left = lax.rem(me + n - 1, n)
    opposite = lax.rem(me + 2, n)
    sides = ((right, left), (left, right))

    def rows(index):
        return pl.ds(pl.multiple_of(index * quarter, quarter), quarter)

    def cols(d):
        return pl.ds(d * half, half)

    def remote(src, dst, send, recv, device):
        return pltpu.make_async_remote_copy(
            src_ref=src, dst_ref=dst, send_sem=send, recv_sem=recv,
            device_id=(group, device), device_id_type=MESH,
        )

    def g_copy(d, stage, j):
        device, origin = sides[d]
        return remote(*(
            (g.at[opposite * each + j, :, cols(d)], fg.at[d, j], g_send.at[d, 0, j], g_recv.at[d, 0, j], device),
            (g.at[device * each + j], gf.at[j, rows(me), :], g_send.at[d, 1, j], g_recv.at[d, 1, j], device),
            (fg.at[d, j], gf.at[j, rows(origin), cols(d)], g_send.at[d, 2, j], g_recv.at[d, 2, j], device),
        )[stage])

    def s_copy(d, stage, j):
        device, origin = sides[d]
        return remote(*(
            (spk.at[opposite * each + j, d], fs.at[d, j], s_send.at[d, 0, j], s_recv.at[d, 0, j], device),
            (spk.at[device * each + j], pk.at[me, j], s_send.at[d, 1, j], s_recv.at[d, 1, j], device),
            (fs.at[d, j], pk.at[origin, j, d], s_send.at[d, 2, j], s_recv.at[d, 2, j], device),
        )[stage])

    def u_copy(d, stage, j):
        device, origin = sides[d]
        return remote(*(
            (upd.at[j, rows(opposite), cols(d)], fu.at[d, j], u_send.at[d, 0, j], u_recv.at[d, 0, j], device),
            (upd.at[j, rows(device), :], update_out.at[me * each + j], u_send.at[d, 1, j], u_recv.at[d, 1, j], device),
            (fu.at[d, j], update_out.at[origin * each + j, :, cols(d)], u_send.at[d, 2, j], u_recv.at[d, 2, j], device),
        )[stage])

    low_lanes = lax.broadcasted_iota(jnp.int32, (quarter, half), 1) < quarter

    def place(value, parity, to):
        return jnp.where(parity == to, value, pltpu.roll(value, quarter, 1))

    def pick(first, second, index, to):
        return place(jnp.where(index // 2 == 0, first, second), lax.rem(index, 2), to)

    class Mirrored:
        def __init__(self, src, dst, packed, passing, landed, send, recv):
            self.src, self.dst, self.packed = src, dst, packed
            self.passing, self.landed, self.send, self.recv = passing, landed, send, recv

        def copy(self, d, stage, j):
            device, origin = sides[d]
            src, dst = (
                (self.packed.at[d, j], self.passing.at[d, j, 0]),
                (self.src.at[:, j, rows(device), :], self.dst.at[:, me * each + j]),
                (self.passing.at[d, j], self.landed.at[d, j]),
            )[stage]
            return remote(src, dst, self.send.at[d, stage, j], self.recv.at[d, stage, j], device)

        def begin(self, j):
            parts = [
                [self.src[i, j, rows(opposite), e * half:(e + 1) * half] for e in (0, 1)]
                for i in (0, 1)
            ]
            for d, index in ((0, me), (1, opposite)):
                self.packed[d, j] = jnp.where(
                    low_lanes, pick(*parts[0], index, 0), pick(*parts[1], index, 1)
                )
            begin(self.copy, j)

        def forward(self, j):
            for d in (0, 1):
                device, origin = sides[d]
                self.copy(d, 0, j).wait_recv()
                self.copy(d, 1, j).wait_recv()
                parts = [
                    pick(
                        self.dst[i, origin * each + j, :, 0:half],
                        self.dst[i, origin * each + j, :, half:extent],
                        device, 0,
                    )
                    for i in (1, 0)
                ]
                self.passing[d, j, 1] = jnp.concatenate(parts, axis=0).T[0:quarter, :]
                self.copy(d, 2, j).start()

        def assemble(self, j):
            for d in (0, 1):
                self.copy(d, 2, j).wait_recv()
            pieces = (
                (self.landed[0, j, 0], opposite, 0),
                (self.landed[0, j, 1], left, 1),
                (self.landed[1, j, 0], me, 0),
                (self.landed[1, j, 1], right, 1),
            )
            for i in (0, 1):
                placed = [
                    (index, place(piece, lax.rem(index, 2), (where + i) % 2))
                    for piece, index, where in pieces
                ]
                for e in (0, 1):
                    part = 2 * e + jnp.where(low_lanes, 0, 1)
                    value = placed[0][1]
                    for index, piece in placed[1:]:
                        value = jnp.where(part == index, piece, value)
                    self.dst[i, opposite * each + j, :, e * half:(e + 1) * half] = value

        def sent(self, j):
            for d in (0, 1):
                for stage in (0, 1, 2):
                    self.copy(d, stage, j).wait_send()

    def begin(copy, j):
        for stage in (0, 1):
            for d in (0, 1):
                copy(d, stage, j).start()

    def forward(copy, j):
        for d in (0, 1):
            copy(d, 0, j).wait_recv()
            copy(d, 2, j).start()

    def arrived(copy, j):
        for d in (0, 1):
            for stage in (1, 2):
                copy(d, stage, j).wait_recv()

    def q_copy(d, stage, j):
        device, origin = sides[d]
        skip = 0 if j % 2 == d else quarter // 2
        return remote(*(
            (gp.at[d, j, skip:quarter], gm.at[d, j, skip:quarter], q_send.at[d, 0, j], q_recv.at[d, 0, j], device),
            (gg.at[1, j, rows(device), :], rg.at[1, me * each + j], q_send.at[d, 1, j], q_recv.at[d, 1, j], device),
            (gm.at[d, j, skip:half], gx.at[d, j, skip:half], q_send.at[d, 2, j], q_recv.at[d, 2, j], device),
            (gd.at[d, j], ga.at[d, j], q_send.at[d, 3, j], q_recv.at[d, 3, j], device),
        )[stage])

    def fold(first, second, index):
        middle = quarter // 2
        return jnp.where(
            low_lanes[0:middle], pick(first, second, index, 0)[0:middle], pick(first, second, index, 1)[middle:]
        )

    def unfold(value):
        return jnp.concatenate([value, pltpu.roll(value, quarter, 1)], axis=0)

    def halves_of(ref, i, block, where):
        return [ref[i, block, where, e * half:(e + 1) * half] for e in (0, 1)]

    def grams_begin(j):
        lefts, rights = halves_of(gg, 0, j, rows(opposite)), halves_of(gg, 1, j, rows(opposite))
        gp[j % 2, j] = jnp.where(low_lanes, pick(*lefts, me, 0), pick(*rights, me, 1))
        gp[1 - j % 2, j, quarter // 2:quarter] = fold(*rights, opposite)
        for d in (0, 1):
            device, origin = sides[d]
            lefts = halves_of(gg, 0, j, rows(device))
            nexts = [lax.rem(device + k, n) for k in (1, 2, 3)]
            gd[d, j, 0:quarter] = jnp.where(low_lanes, pick(*lefts, nexts[0], 0), pick(*lefts, nexts[1], 1))
            gd[d, j, quarter:] = fold(*lefts, nexts[2])
        for stage in (0, 3, 1):
            for d in (0, 1):
                q_copy(d, stage, j).start()

    def grams_forward(j):
        for d in (0, 1):
            device, origin = sides[d]
            for stage in (0, 3, 1):
                q_copy(d, stage, j).wait_recv()
            rights = pick(*halves_of(rg, 1, origin * each + j, slice(None)), device, 0)
            lefts = ga[d, j, 0:quarter] if d == 0 else unfold(ga[d, j, quarter:])
            gm[d, j, quarter:half] = jnp.concatenate([rights, lefts], axis=0).T[0:quarter, :]
            q_copy(d, 2, j).start()

    def put(i, row, pieces):
        placed = [(index, place(piece, lax.rem(index, 2), lane)) for piece, index, lane in pieces]
        for e in (0, 1):
            part = 2 * e + jnp.where(low_lanes, 0, 1)
            value = placed[0][1]
            for index, piece in placed[1:]:
                value = jnp.where(part == index, piece, value)
            rg[i, row, :, e * half:(e + 1) * half] = value

    def own_part(row):
        high, low = split(gown[row])
        def product(x, y):
            return lax.dot_general(
                x, jnp.concatenate([y, y], axis=0), (((1,), (1,)), ((), ())), preferred_element_type=F32
            )
        return product(high, high) + product(high, low) + product(low, high)

    def grams_assemble(j):
        for d in (0, 1):
            q_copy(d, 2, j).wait_recv()
        row = opposite * each + j
        far, middle = gx[j % 2, j, 0:quarter], unfold(gx[1 - j % 2, j, quarter // 2:quarter])
        near = [gx[d, j, quarter:half] for d in (0, 1)]
        put(0, row, ((far, opposite, 0), (near[0], left, 1), (near[1], right, 1), (own_part(row), me, 0)))
        put(1, row, ((far, opposite, 1), (near[0], left, 0), (near[1], right, 0), (middle, me, 0)))
        for d in (0, 1):
            row = sides[d][1] * each + j
            first, third = ga[d, j, 0:quarter], unfold(ga[d, j, quarter:])
            put(0, row, ((first, right, 0), (first, opposite, 1), (third, left, 0), (own_part(row), me, 0)))

    results = Mirrored(out, ro, rp, rm, rx, r_send, r_recv)

    def q_own(j):
        return pltpu.make_async_copy(
            gg.at[:, j, rows(me), :], rg.at[:, me * each + j], own_sem.at[1, j]
        )

    def r_own(j):
        return pltpu.make_async_copy(
            out.at[:, j, rows(me), :], roots_out.at[:, me * each + j], own_sem.at[2, j]
        )

    def u_own(j):
        return pltpu.make_async_copy(
            upd.at[j, rows(me), :], update_out.at[me * each + j], own_sem.at[3, j]
        )

    def keep(owner, j, slot):
        return pltpu.make_async_copy(
            ro.at[:, owner * each + j], roots_out.at[:, owner * each + j], keep_sem.at[slot, j]
        )

    def returned(j):
        results.assemble(j)
        for slot, owner in enumerate((left, right, opposite)):
            keep(owner, j, slot).start()

    def statistics_copy():
        return pltpu.make_async_copy(rg, stats_out, own_sem.at[0, 1])

    def statistics():
        loads[6].wait()
        for j in range(each):
            q_own(j).wait()
            grams_assemble(j)

        @pl.loop(0, blocks)
        def _(b):
            for side in (0, 1):
                rg[side, b] = STAT_DECAY * st[side, b] + (1.0 - STAT_DECAY) * rg[side, b]

        statistics_copy().start()

    loads = [
        pltpu.make_async_copy(ref, place, load_sem.at[i])
        for i, (ref, place) in enumerate(
            ((due, duev), (own, ownv), (ls, st.at[0]), (rs, st.at[1]), (lr, rt.at[0]), (rr, rt.at[1]), (g, gown))
        )
    ]
    own_rows = pltpu.make_async_copy(
        g.at[pl.ds(me * each, each)], gf.at[:, rows(me), :], own_sem.at[0, 0]
    )
    for load in loads:
        load.start()

    barrier = pltpu.get_barrier_semaphore()
    for device in (left, right):
        pl.semaphore_signal(barrier, inc=1, device_id=(group, device), device_id_type=MESH)
    pl.semaphore_wait(barrier, 2)

    begin(g_copy, 0)
    own_rows.start()

    total = own.shape[1]
    for load in loads[:2]:
        load.wait()
    slots = group * blocks + lax.broadcasted_iota(jnp.int32, (blocks, total), 0)
    numbers = lax.broadcasted_iota(jnp.int32, (blocks, total), 1)
    stored = jnp.where(ownv[...] == slots, numbers, 0).astype(F32)
    number = jnp.sum(stored, axis=1, keepdims=True)
    entries = duev[...].astype(F32)
    for side in (0, 1):
        hit = jnp.where(entries == 2.0 * number + side, 1.0, 0.0)
        flag = jnp.max(hit, axis=1, keepdims=True)
        mk[side] = jnp.broadcast_to(flag, (blocks, half))

    for load in loads[2:6]:
        load.wait()

    def choose(j, owner):
        b = owner * each + j
        second = lax.rem(jnp.where(owner == right, me + 2, me + 1), n)
        for side in (0, 1):
            flag = mk[side, pl.ds(b, 1), :] > 0.5
            halves = []
            for d in (0, 1):
                value = jnp.where(
                    flag,
                    st[side, b, :, d * half:(d + 1) * half],
                    rt[side, b, :, d * half:(d + 1) * half],
                )
                sel[side, b, :, d * half:(d + 1) * half] = value
                halves.append(value)
            spk[b, side] = jnp.where(
                low_lanes, pick(*halves, me, 0), pick(*halves, second, 1)
            )

    def choose_all(j):
        @pl.loop(0, n)
        def _(owner):
            choose(j, owner)

    choose_all(0)
    begin(s_copy, 0)
    begin(g_copy, 1)
    choose_all(1)
    forward(g_copy, 0)
    forward(s_copy, 0)
    begin(s_copy, 1)
    for j in range(2, each):
        choose_all(j)
    forward(g_copy, 1)
    forward(s_copy, 1)
    begin(g_copy, 2)
    begin(s_copy, 2)
    own_rows.wait()

    row_ids = lax.broadcasted_iota(jnp.int32, (extent, extent), 0)
    col_ids = lax.broadcasted_iota(jnp.int32, (extent, extent), 1)
    diagonal = row_ids == col_ids
    mat[...] = jnp.zeros_like(mat)
    root[...] = jnp.zeros_like(root)

    def partner(row):
        return lax.rem(row + jnp.where(row == left, 2, 1), n)

    def gram(j):
        arrived(g_copy, j)
        grad = gf[j]
        straight, turned = split(grad), split(grad.T)
        gg[0, j] = mm(straight, turned)
        gg[1, j] = mm(turned, straight)
        grams_begin(j)
        q_own(j).start()

    def prepare(j, chain):
        arrived(s_copy, j)
        row_part, col_part = row_ids // quarter, col_ids // quarter
        other = lax.rem(row_part + jnp.where(row_part == left, 2, 1), n)
        known = (row_part == me) | (row_part == col_part) | (col_part == other)
        for i in (0, 1):
            for row in range(n):
                second = partner(row)
                packed = pk[row, j, i]
                turned_round = pltpu.roll(packed, quarter, 1)
                low = packed if row % 2 == 0 else turned_round
                high = jnp.where(lax.rem(second, 2) == 1, packed, turned_round)
                for d in (0, 1):
                    part = 2 * d + jnp.where(low_lanes, 0, 1)
                    value = jnp.where(part == row, low, jnp.where(part == second, high, 0.0))
                    value = jnp.where(
                        me == row, sel[i, me * each + j, :, d * half:(d + 1) * half], value
                    )
                    spread[i, row * quarter:(row + 1) * quarter, d * half:(d + 1) * half] = value
            whole = spread[i]
            whole = jnp.where(known, whole, whole.T)
            p[i, j] = whole
            chosen = STAT_DECAY * whole + (1.0 - STAT_DECAY) * gg[i, j]
            frobenius = jnp.sqrt(jnp.sum(chosen * chosen, keepdims=True))
            mat[chain + i] = chosen / frobenius
            root[chain + i] = jnp.where(diagonal, 1.0 / jnp.sqrt(jnp.sqrt(frobenius)), 0.0)

    def finish(j, chain):
        for i in (0, 1):
            flag = mk[i, pl.ds(me * each + j, 1), :] > 0.5
            for d in (0, 1):
                out[i, j, :, d * half:(d + 1) * half] = jnp.where(
                    flag,
                    root[chain + i, :, d * half:(d + 1) * half],
                    p[i, j, :, d * half:(d + 1) * half],
                )
        results.begin(j)
        r_own(j).start()
        middle = mm(split(out[0, j]), split(gf[j]))
        upd[j] = mm(split(middle), split(out[1, j]))
        begin(u_copy, j)
        u_own(j).start()

    gram(0)
    prepare(0, 0)
    begin(g_copy, 3)
    begin(s_copy, 3)

    def steps(i):
        factor = jnp.where(diagonal, 1.25, 0.0) - 0.25 * mat[i]
        parts = split(factor)
        yield
        square = mm(parts, parts)
        yield
        parts = split(square)
        rest = split(5.0 * factor - 4.0 * square)
        yield
        fourth = mm(parts, parts)
        yield
        parts = split(fourth)
        yield
        term = mm(parts, rest)
        yield
        joint = split(1.25 * factor - 0.25 * term)
        yield
        square = mm(joint, joint)
        yield
        parts = split(square)
        before = split(root[i])
        yield
        fourth = mm(parts, parts)
        root[i] = mm(before, joint)
        yield
        parts = split(fourth)
        rest = split(mat[i])
        yield
        matrix = mm(parts, rest)
        yield
        mat[i] = matrix
        yield

    def body():
        chains = [steps(i) for i in range(4)]
        waiting = None
        for stage in range(6):
            for chain in chains:
                if stage == 0:
                    next(chain)
                next(chain)
                if waiting is not None:
                    next(waiting)
                waiting = chain
        next(waiting)

    pairs = ITERS // 2

    @pl.loop(0, 2 * pairs + 1)
    def _(t):
        body()

        def at(step, *actions):
            @pl.when(t == step)
            def _():
                for action, *rest in actions:
                    action(*rest)

        @pl.when(t < pairs - 1)
        def _():
            at(0, (forward, g_copy, 2), (forward, s_copy, 2), (gram, 1), (prepare, 1, 2))
            at(1, (forward, g_copy, 3), (forward, s_copy, 3), (gram, 2))
            at(2, (grams_forward, 0), (gram, 3))
            at(3, (grams_forward, 1))

        @pl.when(t >= pairs - 1)
        def _():
            @pl.when(lax.rem(t, pairs) == pairs - 1)
            def _():
                finish(2 * (t // pairs), 0)

            @pl.when(lax.rem(t, pairs) == 0)
            def _():
                finish(2 * (t // pairs) - 1, 2)

            at(pairs - 1, (prepare, 2, 0))
            at(pairs, (prepare, 3, 2), (grams_forward, 2))
            at(6, (grams_forward, 3))
            at(7, (results.forward, 0), (forward, u_copy, 0))
            at(8, (results.forward, 1), (forward, u_copy, 1))

    for j in (2, 3):
        results.forward(j)
        forward(u_copy, j)

    statistics()

    @pl.loop(0, each)
    def _(j):
        returned(j)

    @pl.loop(0, each)
    def _(j):
        for copy in (g_copy, s_copy, u_copy):
            for d in (0, 1):
                for stage in (0, 1, 2):
                    copy(d, stage, j).wait_send()
        results.sent(j)
        arrived(u_copy, j)
        r_own(j).wait()
        u_own(j).wait()
        for slot, owner in enumerate((left, right, opposite)):
            keep(owner, j, slot).wait()

    for j in range(each):
        for d in (0, 1):
            for stage in (0, 1, 2, 3):
                q_copy(d, stage, j).wait_send()
    statistics_copy().wait()


def local(n, gradients, left_stats, right_stats, left_roots, right_roots, due_factors, block_owner):
    blocks, quarter, extent = gradients.shape
    each = blocks // n
    half = extent // 2
    anywhere = pl.BlockSpec(memory_space=pl.ANY)
    dma = pltpu.SemaphoreType.DMA
    words = due_factors.shape[0], block_owner.shape[0]
    stats, roots, update = pl.pallas_call(
        functools.partial(kernel, n),
        out_shape=(
            jax.ShapeDtypeStruct((2, blocks, quarter, extent), F32),
            jax.ShapeDtypeStruct((2, blocks, quarter, extent), F32),
            jax.ShapeDtypeStruct((blocks, quarter, extent), F32),
        ),
        in_specs=[anywhere] * 7,
        out_specs=(anywhere,) * 3,
        scratch_shapes=[
            pltpu.VMEM((1, words[0]), jnp.int32),
            pltpu.VMEM((1, words[1]), jnp.int32),
            pltpu.VMEM((each, extent, extent), F32),
            pltpu.VMEM((2, blocks, quarter, extent), F32),
            pltpu.VMEM((2, blocks, quarter, extent), F32),
            pltpu.VMEM((2, blocks, quarter, extent), F32),
            pltpu.VMEM((blocks, 2, quarter, half), F32),
            pltpu.VMEM((n, each, 2, quarter, half), F32),
            pltpu.VMEM((2, each, extent, extent), F32),
            pltpu.VMEM((2, each, extent, extent), F32),
            pltpu.VMEM((2, blocks, quarter, extent), F32),
            pltpu.VMEM((2, each, extent, extent), F32),
            pltpu.VMEM((2, blocks, quarter, extent), F32),
            pltpu.VMEM((each, extent, extent), F32),
            pltpu.VMEM((2, blocks, half), F32),
            pltpu.VMEM((2, each, quarter, half), F32),
            pltpu.VMEM((2, each, quarter, half), F32),
            pltpu.VMEM((2, each, quarter, half), F32),
            pltpu.VMEM((blocks, quarter, extent), F32),
            pltpu.VMEM((2, each, quarter, half), F32),
            pltpu.VMEM((2, each, 3 * quarter // 2, half), F32),
            pltpu.VMEM((2, each, 3 * quarter // 2, half), F32),
            pltpu.VMEM((2, each, half, half), F32),
            pltpu.VMEM((2, each, half, half), F32),
            pltpu.VMEM((2, each, quarter, half), F32),
            pltpu.VMEM((2, each, 2, quarter, half), F32),
            pltpu.VMEM((2, each, 2, quarter, half), F32),
            pltpu.VMEM((2, extent, extent), F32),
            pltpu.VMEM((4, extent, extent), F32),
            pltpu.VMEM((4, extent, extent), F32),
            dma((7,)),
            dma((4, each)),
            dma((3, each)),
        ] + [dma((2, 3, each))] * 4 + [dma((2, 4, each))] * 2 + [dma((2, 3, each))] * 4,
        compiler_params=pltpu.CompilerParams(
            collective_id=0, has_side_effects=True, vmem_limit_bytes=VMEM_LIMIT
        ),
        cost_estimate=pl.CostEstimate(
            flops=280 * 3 * 2 * extent ** 3, bytes_accessed=10 * 4 * blocks * quarter * extent, transcendentals=0
        ),
    )(
        gradients, left_stats, right_stats, left_roots, right_roots,
        due_factors.reshape(1, -1), block_owner.reshape(1, -1),
    )
    return (stats[0], stats[1], roots[0], roots[1], update)


def solution(mesh):
    spec = P("dp", "shard", None)
    return jax.shard_map(
        functools.partial(local, mesh.shape["shard"]),
        mesh=mesh,
        in_specs=(spec,) * 5 + (P(), P()),
        out_specs=(spec,) * 5,
        check_vma=False,
    )
```
